768 devices in a mesh: row: 48 (over x, z_lo, core), col: 16 (over y, z_hi).
Axes of the slice: x: 4, y: 8, z: 12 (z_hi: 2, z_lo: 6; z = z_hi * 6 + z_lo), core: 2. Of those that a mesh axis runs over, the one named last changes fastest.
Arguments:
- picture_embeds: bfloat16 [196608, 1152], P(('row', 'col')), may hold values from -6 to 6
- caption_embeds: bfloat16 [196608, 1152], P(('row', 'col')), may hold values from -6 to 6
- logit_multiplier: float32 [1], replicated, may hold values from 5 to 20
- offset_shift: float32 [1], replicated, may hold values from -3 to -1
Outputs:
- d_images: float32 [196608, 1152], P(('row', 'col'))
- d_texts: float32 [196608, 1152], P(('row', 'col'))
The draws below stay inside these ranges and needn't reach their ends.
All inputs are finite; a program needn't handle non-finite values.
Results may differ from the reference program's by a relative error of at most 0.0044.
Values may be sent and summed in bfloat16 or wider, within the bound.
No kernel may reach another device: no remote copies, remote signals or barrier semaphores. Data moves between devices by JAX's collectives and lax.ppermute only.
A program may use at most 32 MiB of HBM per device.

```python
import math
import jax
import jax.numpy as jnp
from jax import lax

D = 1152
BLOCK_COUPLES = 256
TOKENS = 196608
N_ROW = 48
N_COL = 16


def level_of(own_key, dims, cuts, least, high):
    def one(dim, blocks):
        draws = jax.random.uniform(jax.random.fold_in(jax.random.fold_in(own_key, 6), dim), (blocks,), jnp.float32, least / len(cuts), high / len(cuts))
        return jnp.repeat(jnp.exp(draws), dims[dim] // blocks).reshape((-1,) + (1,) * (len(dims) - dim - 1))

    gain = one(*cuts[0])
    for cut in cuts[1:]:
        gain = gain * one(*cut)
    return gain


def normal_values(stream_key, dims, width, limit, cuts=(), held_as=jnp.bfloat16):
    loudness = level_of(stream_key, dims, cuts, -0.22, 0.18) if cuts else 1.0
    values = jax.random.normal(stream_key, dims, jnp.float32) * width * loudness
    return jnp.minimum(jnp.maximum(values, -limit), limit).astype(held_as)


def setup_inputs(seed: int = 0) -> dict:
    splits = jax.random.split(jax.random.key(seed), 5)
    return {
        "picture_embeds": normal_values(splits[0], (TOKENS, D), 1.0, 6.0, ((0, 768),)),
        "caption_embeds": normal_values(splits[1], (TOKENS, D), 1.0, 6.0, ((0, 768),)),
        "logit_multiplier": jnp.clip(jnp.exp(jax.random.uniform(splits[2], (1,), jnp.float32, math.log(5.0), math.log(20.0))), 5.0, 20.0),
        "offset_shift": jnp.clip(jax.random.uniform(splits[3], (1,), jnp.float32, -3.0, -1.0), -3.0, -1.0),
    }


def normalize(block):
    values = block.astype(jnp.float32)
    norm = jnp.sqrt(lax.optimization_barrier(jnp.sum(values * values, axis=-1, keepdims=True)) + 1e-06)
    return (values / norm, norm)

def block_coefficient_array(normed_picture_rows, normed_caption_rows, logit_multiplier, offset_shift, target_signs):
    cosine_grid = jnp.einsum('cid,cjd->cij', normed_picture_rows.astype(jnp.float32), normed_caption_rows.astype(jnp.float32))
    similarity_raw = logit_multiplier[0] * cosine_grid + offset_shift[0]
    sigmoid_outputs = jax.nn.sigmoid(similarity_raw)
    if target_signs:
        sigmoid_outputs = sigmoid_outputs - jnp.eye(BLOCK_COUPLES, dtype=jnp.float32)
    return (sigmoid_outputs * (logit_multiplier[0] / BLOCK_COUPLES)).astype(jnp.bfloat16)

def project_back(grad_unit, unit_float, norm):
    inner = lax.optimization_barrier(jnp.sum(unit_float * grad_unit, axis=-1, keepdims=True))
    return (grad_unit - unit_float * inner) / norm

def reference(picture_embeds, caption_embeds, logit_multiplier, offset_shift):
    image_grid = picture_embeds.reshape(N_ROW, N_COL, BLOCK_COUPLES, D)
    text_grid = caption_embeds.reshape(N_ROW, N_COL, BLOCK_COUPLES, D)
    text_before = jnp.roll(text_grid, 1, axis=0)

    def one_row(items):
        image_raw, text_raw, text_prev_raw = items
        image_float, image_norm = normalize(image_raw)
        normed_picture_rows = image_float.astype(jnp.bfloat16)
        text_float, text_norm = normalize(text_raw)
        normed_caption_rows = text_float.astype(jnp.bfloat16)
        prev_float, prev_norm = normalize(text_prev_raw)
        earlier_normed_caption = prev_float.astype(jnp.bfloat16)
        own_normed_caption = jnp.roll(earlier_normed_caption, 1, axis=0)
        leading_summand = block_coefficient_array(normed_picture_rows, normed_caption_rows, logit_multiplier, offset_shift, True)
        middle_summand = block_coefficient_array(normed_picture_rows, earlier_normed_caption, logit_multiplier, offset_shift, False)
        trailing_summand = block_coefficient_array(normed_picture_rows, own_normed_caption, logit_multiplier, offset_shift, False)
        image_f = normed_picture_rows.astype(jnp.float32)
        d_image_unit = jnp.einsum('cij,cjd->cid', leading_summand.astype(jnp.float32), normed_caption_rows.astype(jnp.float32)) + jnp.einsum('cij,cjd->cid', middle_summand.astype(jnp.float32), earlier_normed_caption.astype(jnp.float32)) + jnp.einsum('cij,cjd->cid', trailing_summand.astype(jnp.float32), own_normed_caption.astype(jnp.float32))
        own_text = jnp.einsum('cij,cid->cjd', leading_summand.astype(jnp.float32), image_f)
        term_prev = jnp.einsum('cij,cid->cjd', middle_summand.astype(jnp.float32), image_f)
        term_diag = jnp.einsum('cij,cid->cjd', trailing_summand.astype(jnp.float32), image_f)
        carried = term_prev + jnp.roll(term_diag, -1, axis=0)
        d_image = project_back(d_image_unit, image_float, image_norm)
        return (d_image, own_text, carried)
    d_image, own_text, carried = lax.map(one_row, (image_grid, text_grid, text_before))
    d_text_unit = own_text + jnp.roll(carried, -1, axis=0)
    text_float, text_norm = normalize(text_grid)
    d_text = project_back(d_text_unit, text_float, text_norm)
    return (d_image.reshape(TOKENS, D), d_text.reshape(TOKENS, D))
```

```python
import jax
import jax.numpy as jnp
from jax import lax
from jax.sharding import PartitionSpec as P

BLOCK_COUPLES = 256
AXES = ("row", "col")


def moved(block, rows_on, cols_on):
    n_row, n_col = (lax.axis_size(a) for a in AXES)
    route = [
        (r * n_col + c, (r + rows_on) % n_row * n_col + (c + cols_on) % n_col)
        for r in range(n_row)
        for c in range(n_col)
    ]
    return lax.ppermute(block, AXES, route)


def normalize(block):
    values = block.astype(jnp.float32)
    norm = jnp.sqrt(jnp.sum(values * values, axis=-1, keepdims=True) + 1e-06)
    return (values / norm, norm)


def unit(block):
    return normalize(block)[0].astype(jnp.bfloat16)


def weights_of(left, right, logit_multiplier, offset_shift, matched):
    cosine = lax.dot_general(
        left, right, (((1,), (1,)), ((), ())), preferred_element_type=jnp.float32
    )
    share = jax.nn.sigmoid(logit_multiplier[0] * cosine + offset_shift[0])
    if matched:
        share = share - jnp.eye(BLOCK_COUPLES, dtype=jnp.float32)
    return (share * (logit_multiplier[0] / BLOCK_COUPLES)).astype(jnp.bfloat16)


def project_back(grad_unit, unit_float, norm):
    inner = jnp.sum(unit_float * grad_unit, axis=-1, keepdims=True)
    return (grad_unit - unit_float * inner) / norm


def per_device(picture_embeds, caption_embeds, logit_multiplier, offset_shift):
    text_diag = moved(caption_embeds, 1, 1)
    image_diag = moved(picture_embeds, -1, -1)
    text_before = moved(caption_embeds, 1, 0)
    image_after = moved(picture_embeds, -1, 0)

    def side(own, others, other_own, matched):
        grad = None
        own_unit = unit(own)
        for k, other in enumerate([other_own, *others]):
            other_unit = unit(other)
            weights = weights_of(own_unit, other_unit, logit_multiplier, offset_shift, k == 0)
            term = jnp.dot(weights, other_unit, preferred_element_type=jnp.float32)
            grad = term if grad is None else grad + term
        return project_back(grad, *normalize(own))

    d_images = side(picture_embeds, [text_before, text_diag], caption_embeds, True)
    d_texts = side(caption_embeds, [image_after, image_diag], picture_embeds, True)
    return (d_images, d_texts)


def solution(mesh):
    placed = (P(("row", "col"), None), P(("row", "col"), None), P(), P())
    return jax.shard_map(
        per_device,
        mesh=mesh,
        in_specs=placed,
        out_specs=(P(("row", "col"), None), P(("row", "col"), None)),
        check_vma=False,
    )
```

```python
import functools

import jax
import jax.numpy as jnp
from jax import lax
from jax.experimental import pallas as pl
from jax.experimental.pallas import tpu as pltpu
from jax.sharding import PartitionSpec as P

AXES = ("row", "col")


def moved(block, rows_on, cols_on):
    n_row, n_col = (lax.axis_size(a) for a in AXES)
    route = [
        (r * n_col + c, (r + rows_on) % n_row * n_col + (c + cols_on) % n_col)
        for r in range(n_row)
        for c in range(n_col)
    ]
    return lax.ppermute(block, AXES, route)


def inverse_norm(values):
    return 1.0 / jnp.sqrt(jnp.sum(values * values, axis=-1, keepdims=True) + 1e-06)


def unit(block):
    values = block.astype(jnp.float32)
    return (values * inverse_norm(values)).astype(jnp.bfloat16)


def weights_of(left, right, multiplier, shift, matched):
    cosine = lax.dot_general(
        left, right, (((1,), (1,)), ((), ())), preferred_element_type=jnp.float32
    )
    share = 1.0 / (1.0 + jnp.exp(-(multiplier * cosine + shift)))
    if matched:
        at = [lax.broadcasted_iota(jnp.int32, share.shape, d) for d in (0, 1)]
        share = jnp.where(at[0] == at[1], share - 1.0, share)
    return (share * (multiplier / left.shape[0])).astype(jnp.bfloat16)


def own_kernel(multiplier, shift, image, text, d_image, d_text):
    image_unit, text_unit = unit(image[...]), unit(text[...])
    for own, other, out in ((image_unit, text_unit, d_image), (text_unit, image_unit, d_text)):
        weights = weights_of(own, other, multiplier[0], shift[0], True)
        out[...] = jnp.dot(weights, other, preferred_element_type=jnp.float32)


def side_kernel(multiplier, shift, far, near, own, start, out, total, sems):
    rows = own.shape[0]
    values = own[...].astype(jnp.float32)
    inverse = inverse_norm(values)
    own_unit = (values * inverse).astype(jnp.bfloat16)
    grad = start[...]
    for block in (near, far):
        other = unit(block[...])
        weights = weights_of(own_unit, other, multiplier[0], shift[0], False)
        grad = grad + jnp.dot(weights, other, preferred_element_type=jnp.float32)
    total[...] = grad
    parts = sems.shape[0]
    copies = []
    for i in range(parts):
        part = slice(i * rows // parts, (i + 1) * rows // parts)
        own_float = own[part].astype(jnp.float32) * inverse[part]
        grad = total[part]
        inner = jnp.sum(own_float * grad, axis=-1, keepdims=True)
        total[part] = (grad - own_float * inner) * inverse[part]
        copy = pltpu.make_async_copy(total.at[part], out.at[part], sems.at[i])
        copy.start()
        copies.append(copy)
    for copy in copies:
        copy.wait()


SCALAR = pl.BlockSpec(memory_space=pltpu.SMEM)
WHOLE = pl.BlockSpec(memory_space=pltpu.VMEM)
PARAMS = pltpu.CompilerParams(vmem_limit_bytes=32 << 20)
PARTS = 4


def own_call(*operands):
    grad = jax.ShapeDtypeStruct(operands[-1].shape, jnp.float32)
    return pl.pallas_call(
        own_kernel,
        out_shape=(grad, grad),
        in_specs=[SCALAR] * 2 + [WHOLE] * 2,
        out_specs=[WHOLE] * 2,
        compiler_params=PARAMS,
        name="own",
    )(*operands)


def side_call(*operands):
    grad = jax.ShapeDtypeStruct(operands[-1].shape, jnp.float32)
    return pl.pallas_call(
        side_kernel,
        out_shape=grad,
        in_specs=[SCALAR] * 2 + [WHOLE] * 4,
        out_specs=pl.BlockSpec(memory_space=pl.ANY),
        scratch_shapes=[
            pltpu.VMEM(grad.shape, jnp.float32),
            pltpu.SemaphoreType.DMA((PARTS,)),
        ],
        compiler_params=PARAMS,
        name="side",
    )(*operands)


def per_device(picture_embeds, caption_embeds, logit_multiplier, offset_shift):
    scalars = (logit_multiplier, offset_shift)
    text_far = moved(caption_embeds, 1, 1)
    image_far = moved(picture_embeds, -1, -1)
    text_near = moved(caption_embeds, 1, 0)
    image_near = moved(picture_embeds, -1, 0)
    image_start, text_start = own_call(*scalars, picture_embeds, caption_embeds)
    d_images = side_call(*scalars, text_far, text_near, picture_embeds, image_start)
    d_texts = side_call(*scalars, image_far, image_near, caption_embeds, text_start)
    return (d_images, d_texts)


def solution(mesh):
    placed = (P(("row", "col"), None), P(("row", "col"), None), P(), P())
    return jax.shard_map(
        per_device,
        mesh=mesh,
        in_specs=placed,
        out_specs=(P(("row", "col"), None), P(("row", "col"), None)),
        check_vma=False,
    )
```

```python
import jax
import jax.numpy as jnp
from jax import lax
from jax.experimental import pallas as pl
from jax.experimental.pallas import tpu as pltpu
from jax.sharding import PartitionSpec as P

AXES = ("row", "col")
FIRST = 0
WIDTH = 256


def swapped(block, cols_on, parity, columns=None):
    n_row, n_col = (lax.axis_size(a) for a in AXES)
    route = []
    for r in range(parity, n_row, 2):
        for c in range(n_col):
            if columns is not None and c % 2 != columns:
                continue
            here = r * n_col + c
            there = (r + 1) % n_row * n_col + (c + cols_on) % n_col
            route += [(here, there), (there, here)]
    return lax.ppermute(block, AXES, route)


def inverse_norm(values):
    return 1.0 / jnp.sqrt(jnp.sum(values * values, axis=-1, keepdims=True) + 1e-06)


def unit(block):
    values = block.astype(jnp.float32)
    return (values * inverse_norm(values)).astype(jnp.bfloat16)


def cosines(left, right):
    return lax.dot_general(
        left, right, (((1,), (1,)), ((), ())), preferred_element_type=jnp.float32
    )


def weights_of(cosine, multiplier, shift, matched=False):
    share = 1.0 / (1.0 + jnp.exp(-(multiplier[0] * cosine + shift[0])))
    if matched:
        at = [lax.broadcasted_iota(jnp.int32, share.shape, d) for d in (0, 1)]
        share = jnp.where(at[0] == at[1], share - 1.0, share)
    return (share * (multiplier[0] / cosine.shape[0])).astype(jnp.bfloat16)


def tile_sum(own_unit, other_unit, multiplier, shift, matched=False):
    weights = weights_of(cosines(own_unit, other_unit), multiplier, shift, matched)
    return jnp.dot(weights, other_unit, preferred_element_type=jnp.float32)


def own_kernel(multiplier, shift, first, second, near, *outs):
    d_first, d_second, own_unit, rest, inverse_out, inner_out = outs
    first_unit = unit(first[...])
    values = second[...].astype(jnp.float32)
    inverse = inverse_norm(values)
    own_float = values * inverse
    second_unit = own_float.astype(jnp.bfloat16)
    d_first[...] = tile_sum(first_unit, second_unit, multiplier, shift, True)
    grad = tile_sum(second_unit, first_unit, multiplier, shift, True) + tile_sum(
        second_unit, unit(near[...]), multiplier, shift
    )
    d_second[...] = grad
    own_unit[...] = second_unit
    rest[...] = (own_float - second_unit.astype(jnp.float32)).astype(jnp.bfloat16)
    inverse_out[...] = jnp.broadcast_to(inverse, inverse_out.shape)
    inner = jnp.sum(own_float * grad, axis=-1, keepdims=True)
    inner_out[...] = jnp.broadcast_to(inner, inner_out.shape)


def parts_of(width):
    return [slice(a, min(a + WIDTH, width)) for a in range(0, width, WIDTH)]


def write_out(action, parts, total, outs, chosen, sems):
    for i, out in enumerate(outs):

        @pl.when(chosen == i)
        def _():
            for k, part in parts:
                copy = pltpu.make_async_copy(total.at[:, part], out.at[:, part], sems.at[k])
                getattr(copy, action)()


def first_kernel(multiplier, shift, odd, own, start, far, near, d_images, d_texts, total, sems):
    values = own[...].astype(jnp.float32)
    inverse = inverse_norm(values)
    own_float = values * inverse
    own_unit = own_float.astype(jnp.bfloat16)
    grad = start[...]
    for block in (far, near):
        grad += tile_sum(own_unit, unit(block[...]), multiplier, shift)
    inner = jnp.sum(own_float * grad, axis=-1, keepdims=True)
    total[...] = (grad - own_float * inner) * inverse
    parts = list(enumerate(parts_of(own.shape[1])))
    image_side = jnp.where(odd[0] == FIRST, 0, 1)
    for action in ("start", "wait"):
        write_out(action, parts, total, (d_texts, d_images), image_side, sems)


def second_kernel(
    multiplier, shift, odd, late, own, start, own_unit, rest, inverse, inner, far, near, *refs
):
    d_images, d_texts, far_unit, near_sum, total, sems = refs[-6:]
    far_unit[...] = unit(far[...])
    cosine = cosines(own_unit[...], far_unit[...])
    weights = weights_of(cosine, multiplier, shift)
    exact = cosine + cosines(rest[...], far_unit[...])
    scale = inverse[:, :1]
    far_inner = inner[:, :1] + jnp.sum(
        weights.astype(jnp.float32) * exact, axis=-1, keepdims=True
    )
    parts = list(enumerate(parts_of(own.shape[1])))
    text_side = jnp.where(odd[0] == FIRST, 0, 1)

    def finish(begun, inner):
        inner = inner * scale
        for k, part in parts:
            grad = begun[:, part] + jnp.dot(
                weights, far_unit[:, part], preferred_element_type=jnp.float32
            )
            own_float = own[:, part].astype(jnp.float32) * scale
            total[:, part] = grad * scale - own_float * inner
            write_out("start", [(k, part)], total, (d_images, d_texts), text_side, sems)
        write_out("wait", parts, total, (d_images, d_texts), text_side, sems)

    @pl.when(late[0] == 0)
    def _():
        finish(start, far_inner)

    @pl.when(late[0] == 1)
    def _():
        grad = tile_sum(own_unit[...], unit(near[...]), multiplier, shift)
        near_sum[...] = start[...] + grad
        own_float = own[...].astype(jnp.float32) * scale
        finish(near_sum, far_inner + jnp.sum(own_float * grad, axis=-1, keepdims=True))


SCALAR = pl.BlockSpec(memory_space=pltpu.SMEM)
WHOLE = pl.BlockSpec(memory_space=pltpu.VMEM)
ANYWHERE = pl.BlockSpec(memory_space=pl.ANY)
PARAMS = pltpu.CompilerParams(vmem_limit_bytes=32 << 20)


def own_call(multiplier, shift, first, second, near):
    grad = jax.ShapeDtypeStruct(first.shape, jnp.float32)
    block = jax.ShapeDtypeStruct(first.shape, jnp.bfloat16)
    column = jax.ShapeDtypeStruct((first.shape[0], 128), jnp.float32)
    return pl.pallas_call(
        own_kernel,
        out_shape=(grad, grad, block, block, column, column),
        in_specs=[SCALAR] * 2 + [WHOLE] * 3,
        out_specs=[WHOLE] * 6,
        compiler_params=PARAMS,
        name="own",
    )(multiplier, shift, first, second, near)


def side_call(kernel, scalars, blocks, held, scratch, name):
    shape = blocks[0].shape
    grad = jax.ShapeDtypeStruct(shape, jnp.float32)
    operands = (*scalars, *blocks)
    return pl.pallas_call(
        kernel,
        out_shape=(grad, grad),
        in_specs=[SCALAR] * len(scalars) + [WHOLE] * len(blocks) + [ANYWHERE] * len(held),
        out_specs=[ANYWHERE] * 2,
        input_output_aliases={len(operands) + i: i for i in range(len(held))},
        scratch_shapes=[
            *(pltpu.VMEM(shape, dtype) for dtype in scratch),
            pltpu.VMEM(shape, jnp.float32),
            pltpu.SemaphoreType.DMA((len(parts_of(shape[1])),)),
        ],
        compiler_params=PARAMS,
        name=name,
    )(*operands, *held)


def per_device(picture_embeds, caption_embeds, logit_multiplier, offset_shift):
    scalars = (logit_multiplier, offset_shift)
    odd, late = ((lax.axis_index(a) % 2).astype(jnp.int32)[None] for a in AXES)
    first = jnp.where(odd == FIRST, caption_embeds, picture_embeds)
    second = jnp.where(odd == FIRST, picture_embeds, caption_embeds)
    early_near = swapped(second, 0, 1 - FIRST, 0)
    first_far, first_near = swapped(first, 1, FIRST), swapped(first, 0, FIRST)
    second_far = swapped(second, 1, 1 - FIRST)
    late_near = swapped(second, 0, 1 - FIRST, 1)
    first_start, *second_own = own_call(*scalars, first, second, early_near)
    held = side_call(
        first_kernel,
        (*scalars, odd),
        (first, first_start, first_far, first_near),
        (),
        (),
        "first",
    )
    return side_call(
        second_kernel,
        (*scalars, odd, late),
        (second, *second_own, second_far, late_near),
        held,
        (jnp.bfloat16, jnp.float32),
        "second",
    )


def solution(mesh):
    placed = (P(("row", "col"), None), P(("row", "col"), None), P(), P())
    return jax.shard_map(
        per_device,
        mesh=mesh,
        in_specs=placed,
        out_specs=(P(("row", "col"), None), P(("row", "col"), None)),
        check_vma=False,
    )
```

```python
import jax
import jax.numpy as jnp
from jax import lax
from jax.experimental import pallas as pl
from jax.experimental.pallas import tpu as pltpu
from jax.sharding import PartitionSpec as P

AXES = ("row", "col")
WIDTH = 256


def moved(block, way):
    n_row, n_col = (lax.axis_size(a) for a in AXES)
    route = []
    for r in range(n_row):
        for c in range(n_col):
            on = way(r, c)
            if on is not None:
                there = (r + on[0]) % n_row * n_col + (c + on[1]) % n_col
                route.append((r * n_col + c, there))
    return lax.ppermute(block, AXES, route)


def inverse_norm(values):
    return 1.0 / jnp.sqrt(jnp.sum(values * values, axis=-1, keepdims=True) + 1e-06)


def unit(block):
    values = block.astype(jnp.float32)
    return (values * inverse_norm(values)).astype(jnp.bfloat16)


def cosines(left, right):
    return lax.dot_general(
        left, right, (((1,), (1,)), ((), ())), preferred_element_type=jnp.float32
    )


def weights_of(cosine, multiplier, shift, matched=False):
    share = 1.0 / (1.0 + jnp.exp(-(multiplier[0] * cosine + shift[0])))
    if matched:
        at = [lax.broadcasted_iota(jnp.int32, share.shape, d) for d in (0, 1)]
        share = jnp.where(at[0] == at[1], share - 1.0, share)
    return (share * (multiplier[0] / cosine.shape[0])).astype(jnp.bfloat16)


def tile_sum(own_unit, other_unit, multiplier, shift, matched=False):
    weights = weights_of(cosines(own_unit, other_unit), multiplier, shift, matched)
    return jnp.dot(weights, other_unit, preferred_element_type=jnp.float32)


def own_kernel(multiplier, shift, odd, first, second, moved_text, *outs):
    d_first, d_second, own_unit, rest, inverse_out, inner_out = outs
    first_unit = unit(first[...])
    values = second[...].astype(jnp.float32)
    inverse = inverse_norm(values)
    own_float = values * inverse
    second_unit = own_float.astype(jnp.bfloat16)
    other_unit = unit(moved_text[...])
    d_first[...] = tile_sum(first_unit, second_unit, multiplier, shift, True)
    d_second[...] = tile_sum(second_unit, first_unit, multiplier, shift, True)

    @pl.when(odd[0] == 1)
    def _():
        d_first[...] += tile_sum(first_unit, other_unit, multiplier, shift)

    @pl.when(odd[0] == 0)
    def _():
        d_second[...] += tile_sum(second_unit, other_unit, multiplier, shift)

    own_unit[...] = second_unit
    rest[...] = (own_float - second_unit.astype(jnp.float32)).astype(jnp.bfloat16)
    inverse_out[...] = jnp.broadcast_to(inverse, inverse_out.shape)
    inner = jnp.sum(own_float * d_second[...], axis=-1, keepdims=True)
    inner_out[...] = jnp.broadcast_to(inner, inner_out.shape)


def parts_of(width):
    return [slice(a, min(a + WIDTH, width)) for a in range(0, width, WIDTH)]


def write_out(action, parts, total, outs, chosen, sems):
    for i, out in enumerate(outs):

        @pl.when(chosen == i)
        def _():
            for k, part in parts:
                copy = pltpu.make_async_copy(total.at[:, part], out.at[:, part], sems.at[k])
                getattr(copy, action)()


def image_kernel(
    multiplier, shift, odd, moved_image, first, first_start, second, second_start, second_unit,
    second_inverse, second_inner, first_sum, second_sum, inner_out
):
    other_unit = unit(moved_image[...])

    @pl.when(odd[0] == 0)
    def _():
        first_sum[...] = first_start[...] + tile_sum(
            unit(first[...]), other_unit, multiplier, shift
        )
        second_sum[...] = second_start[...]
        inner_out[...] = second_inner[...]

    @pl.when(odd[0] == 1)
    def _():
        grad = tile_sum(second_unit[...], other_unit, multiplier, shift)
        first_sum[...] = first_start[...]
        second_sum[...] = second_start[...] + grad
        second_float = second[...].astype(jnp.float32) * second_inverse[:, :1]
        inner_out[...] = second_inner[...] + jnp.sum(second_float * grad, axis=-1, keepdims=True)


def first_kernel(multiplier, shift, odd, own, start, near, d_images, d_texts, total, sems):
    values = own[...].astype(jnp.float32)
    inverse = inverse_norm(values)
    own_float = values * inverse
    own_unit = own_float.astype(jnp.bfloat16)
    grad = start[...] + tile_sum(own_unit, unit(near[...]), multiplier, shift)
    inner = jnp.sum(own_float * grad, axis=-1, keepdims=True)
    total[...] = (grad - own_float * inner) * inverse
    parts = list(enumerate(parts_of(own.shape[1])))
    for action in ("start", "wait"):
        write_out(action, parts, total, (d_texts, d_images), odd[0], sems)


def second_kernel(
    multiplier, shift, odd, late, own, start, own_unit, rest, inverse, inner, far, near, *refs
):
    d_images, d_texts, far_unit, near_sum, total, sems = refs[-6:]
    far_unit[...] = unit(far[...])
    cosine = cosines(own_unit[...], far_unit[...])
    weights = weights_of(cosine, multiplier, shift)
    exact = cosine + cosines(rest[...], far_unit[...])
    scale = inverse[:, :1]
    far_inner = inner[:, :1] + jnp.sum(
        weights.astype(jnp.float32) * exact, axis=-1, keepdims=True
    )
    parts = list(enumerate(parts_of(own.shape[1])))
    text_side = jnp.where(odd[0] == 0, 0, 1)

    def finish(begun, inner):
        inner = inner * scale
        for k, part in parts:
            grad = begun[:, part] + jnp.dot(
                weights, far_unit[:, part], preferred_element_type=jnp.float32
            )
            own_float = own[:, part].astype(jnp.float32) * scale
            total[:, part] = grad * scale - own_float * inner
            write_out("start", [(k, part)], total, (d_images, d_texts), text_side, sems)
        write_out("wait", parts, total, (d_images, d_texts), text_side, sems)

    @pl.when(late[0] == 0)
    def _():
        finish(start, far_inner)

    @pl.when(late[0] == 1)
    def _():
        grad = tile_sum(own_unit[...], unit(near[...]), multiplier, shift)
        near_sum[...] = start[...] + grad
        own_float = own[...].astype(jnp.float32) * scale
        finish(near_sum, far_inner + jnp.sum(own_float * grad, axis=-1, keepdims=True))


SCALAR = pl.BlockSpec(memory_space=pltpu.SMEM)
WHOLE = pl.BlockSpec(memory_space=pltpu.VMEM)
ANYWHERE = pl.BlockSpec(memory_space=pl.ANY)
PARAMS = pltpu.CompilerParams(vmem_limit_bytes=32 << 20)


def own_call(multiplier, shift, odd, first, second, moved_text):
    grad = jax.ShapeDtypeStruct(first.shape, jnp.float32)
    block = jax.ShapeDtypeStruct(first.shape, jnp.bfloat16)
    column = jax.ShapeDtypeStruct((first.shape[0], 128), jnp.float32)
    return pl.pallas_call(
        own_kernel,
        out_shape=(grad, grad, block, block, column, column),
        in_specs=[SCALAR] * 3 + [WHOLE] * 3,
        out_specs=[WHOLE] * 6,
        compiler_params=PARAMS,
        name="own",
    )(multiplier, shift, odd, first, second, moved_text)


def image_call(multiplier, shift, odd, *blocks):
    sums = (blocks[2], blocks[4], blocks[7])
    return pl.pallas_call(
        image_kernel,
        out_shape=tuple(jax.ShapeDtypeStruct(x.shape, x.dtype) for x in sums),
        in_specs=[SCALAR] * 3 + [WHOLE] * len(blocks),
        out_specs=[WHOLE] * 3,
        compiler_params=PARAMS,
        name="image",
    )(multiplier, shift, odd, *blocks)


def side_call(kernel, scalars, blocks, held, scratch, name):
    shape = blocks[0].shape
    grad = jax.ShapeDtypeStruct(shape, jnp.float32)
    operands = (*scalars, *blocks)
    return pl.pallas_call(
        kernel,
        out_shape=(grad, grad),
        in_specs=[SCALAR] * len(scalars) + [WHOLE] * len(blocks) + [ANYWHERE] * len(held),
        out_specs=[ANYWHERE] * 2,
        input_output_aliases={len(operands) + i: i for i in range(len(held))},
        scratch_shapes=[
            *(pltpu.VMEM(shape, dtype) for dtype in scratch),
            pltpu.VMEM(shape, jnp.float32),
            pltpu.SemaphoreType.DMA((len(parts_of(shape[1])),)),
        ],
        compiler_params=PARAMS,
        name=name,
    )(*operands, *held)


def per_device(picture_embeds, caption_embeds, logit_multiplier, offset_shift):
    scalars = (logit_multiplier, offset_shift)
    odd, late = ((lax.axis_index(a) % 2).astype(jnp.int32)[None] for a in AXES)
    text_moved = moved(
        caption_embeds, lambda r, c: (1, 1) if r % 2 == 0 else (1, 0) if c % 2 == 0 else None
    )
    image_moved = moved(
        picture_embeds, lambda r, c: (-1, -1) if r % 2 else (-1, 0) if c % 2 == 0 else None
    )
    first = jnp.where(odd == 0, caption_embeds, picture_embeds)
    second = jnp.where(odd == 0, picture_embeds, caption_embeds)
    first_near = moved(first, lambda r, c: (-1, 0) if r % 2 else (1, 0))
    second_far = moved(second, lambda r, c: (1, 1) if r % 2 else (-1, -1))
    late_near = moved(second, lambda r, c: None if c % 2 == 0 else (1, 0) if r % 2 else (-1, 0))
    first_start, second_start, second_unit, rest, inverse, inner = own_call(
        *scalars, odd, first, second, text_moved
    )
    first_sum, second_sum, inner = image_call(
        *scalars, odd, image_moved, first, first_start,
        second, second_start, second_unit, inverse, inner,
    )
    held = side_call(
        first_kernel, (*scalars, odd), (first, first_sum, first_near), (), (), "first"
    )
    return side_call(
        second_kernel,
        (*scalars, odd, late),
        (second, second_sum, second_unit, rest, inverse, inner, second_far, late_near),
        held,
        (jnp.bfloat16, jnp.float32),
        "second",
    )


def solution(mesh):
    placed = (P(("row", "col"), None), P(("row", "col"), None), P(), P())
    return jax.shard_map(
        per_device,
        mesh=mesh,
        in_specs=placed,
        out_specs=(P(("row", "col"), None), P(("row", "col"), None)),
        check_vma=False,
    )
```

```python
import jax
import jax.numpy as jnp
from jax import lax
from jax.experimental import pallas as pl
from jax.experimental.pallas import tpu as pltpu
from jax.sharding import PartitionSpec as P

AXES = ("row", "col")
FIRST = 0
WIDTH = 128


def swapped(block, cols_on, parity, columns=None):
    n_row, n_col = (lax.axis_size(a) for a in AXES)
    route = []
    for r in range(parity, n_row, 2):
        for c in range(n_col):
            if columns is not None and c % 2 != columns:
                continue
            here = r * n_col + c
            there = (r + 1) % n_row * n_col + (c + cols_on) % n_col
            route += [(here, there), (there, here)]
    return lax.ppermute(block, AXES, route)


def inverse_norm(values):
    return 1.0 / jnp.sqrt(jnp.sum(values * values, axis=-1, keepdims=True) + 1e-06)


def unit(block):
    values = block.astype(jnp.float32)
    return (values * inverse_norm(values)).astype(jnp.bfloat16)


def cosines(left, right):
    return lax.dot_general(
        left, right, (((1,), (1,)), ((), ())), preferred_element_type=jnp.float32
    )


def weights_of(cosine, multiplier, shift, matched=False):
    share = 1.0 / (1.0 + jnp.exp(-(multiplier[0] * cosine + shift[0])))
    if matched:
        at = [lax.broadcasted_iota(jnp.int32, share.shape, d) for d in (0, 1)]
        share = jnp.where(at[0] == at[1], share - 1.0, share)
    return (share * (multiplier[0] / cosine.shape[0])).astype(jnp.bfloat16)


def tile_sum(own_unit, other_unit, multiplier, shift, matched=False):
    weights = weights_of(cosines(own_unit, other_unit), multiplier, shift, matched)
    return jnp.dot(weights, other_unit, preferred_element_type=jnp.float32)


def own_kernel(multiplier, shift, first, second, near, *outs):
    d_first, d_second, own_unit, rest, inverse_out, inner_out = outs
    first_unit = unit(first[...])
    values = second[...].astype(jnp.float32)
    inverse = inverse_norm(values)
    own_float = values * inverse
    second_unit = own_float.astype(jnp.bfloat16)
    d_first[...] = tile_sum(first_unit, second_unit, multiplier, shift, True)
    grad = tile_sum(second_unit, first_unit, multiplier, shift, True) + tile_sum(
        second_unit, unit(near[...]), multiplier, shift
    )
    d_second[...] = grad
    own_unit[...] = second_unit
    rest[...] = (own_float - second_unit.astype(jnp.float32)).astype(jnp.bfloat16)
    inverse_out[...] = jnp.broadcast_to(inverse, inverse_out.shape)
    inner = jnp.sum(own_float * grad, axis=-1, keepdims=True)
    inner_out[...] = jnp.broadcast_to(inner, inner_out.shape)


def parts_of(width):
    return [slice(a, min(a + WIDTH, width)) for a in range(0, width, WIDTH)]


def write_out(action, parts, total, outs, chosen, sems):
    for i, out in enumerate(outs):

        @pl.when(chosen == i)
        def _():
            for k, part in parts:
                copy = pltpu.make_async_copy(total.at[:, part], out.at[:, part], sems.at[k])
                getattr(copy, action)()


def first_kernel(multiplier, shift, odd, own, start, far, near, d_images, d_texts, total, sems):
    values = own[...].astype(jnp.float32)
    inverse = inverse_norm(values)
    own_float = values * inverse
    own_unit = own_float.astype(jnp.bfloat16)
    grad = start[...]
    for block in (far, near):
        grad += tile_sum(own_unit, unit(block[...]), multiplier, shift)
    inner = jnp.sum(own_float * grad, axis=-1, keepdims=True)
    total[...] = (grad - own_float * inner) * inverse
    parts = list(enumerate(parts_of(own.shape[1])))
    image_side = jnp.where(odd[0] == FIRST, 0, 1)
    for action in ("start", "wait"):
        write_out(action, parts, total, (d_texts, d_images), image_side, sems)


def second_kernel(
    multiplier, shift, odd, late, own, start, own_unit, rest, inverse, inner, far, near, *refs
):
    d_images, d_texts, far_unit, near_sum, total, sems = refs[-6:]
    far_unit[...] = unit(far[...])
    cosine = cosines(own_unit[...], far_unit[...])
    weights = weights_of(cosine, multiplier, shift)
    exact = cosine + cosines(rest[...], far_unit[...])
    scale = inverse[:, :1]
    far_inner = inner[:, :1] + jnp.sum(
        weights.astype(jnp.float32) * exact, axis=-1, keepdims=True
    )
    parts = list(enumerate(parts_of(own.shape[1])))
    text_side = jnp.where(odd[0] == FIRST, 0, 1)

    def finish(begun, inner):
        inner = inner * scale
        for k, part in parts:
            grad = begun[:, part] + jnp.dot(
                weights, far_unit[:, part], preferred_element_type=jnp.float32
            )
            own_float = own[:, part].astype(jnp.float32) * scale
            total[:, part] = grad * scale - own_float * inner
            write_out("start", [(k, part)], total, (d_images, d_texts), text_side, sems)
        write_out("wait", parts, total, (d_images, d_texts), text_side, sems)

    @pl.when(late[0] == 0)
    def _():
        finish(start, far_inner)

    @pl.when(late[0] == 1)
    def _():
        grad = tile_sum(own_unit[...], unit(near[...]), multiplier, shift)
        near_sum[...] = start[...] + grad
        own_float = own[...].astype(jnp.float32) * scale
        finish(near_sum, far_inner + jnp.sum(own_float * grad, axis=-1, keepdims=True))


SCALAR = pl.BlockSpec(memory_space=pltpu.SMEM)
WHOLE = pl.BlockSpec(memory_space=pltpu.VMEM)
ANYWHERE = pl.BlockSpec(memory_space=pl.ANY)
PARAMS = pltpu.CompilerParams(vmem_limit_bytes=32 << 20)


def own_call(multiplier, shift, first, second, near):
    grad = jax.ShapeDtypeStruct(first.shape, jnp.float32)
    block = jax.ShapeDtypeStruct(first.shape, jnp.bfloat16)
    column = jax.ShapeDtypeStruct((first.shape[0], 128), jnp.float32)
    return pl.pallas_call(
        own_kernel,
        out_shape=(grad, grad, block, block, column, column),
        in_specs=[SCALAR] * 2 + [WHOLE] * 3,
        out_specs=[WHOLE] * 6,
        compiler_params=PARAMS,
        name="own",
    )(multiplier, shift, first, second, near)


def side_call(kernel, scalars, blocks, held, scratch, name):
    shape = blocks[0].shape
    grad = jax.ShapeDtypeStruct(shape, jnp.float32)
    operands = (*scalars, *blocks)
    return pl.pallas_call(
        kernel,
        out_shape=(grad, grad),
        in_specs=[SCALAR] * len(scalars) + [WHOLE] * len(blocks) + [ANYWHERE] * len(held),
        out_specs=[ANYWHERE] * 2,
        input_output_aliases={len(operands) + i: i for i in range(len(held))},
        scratch_shapes=[
            *(pltpu.VMEM(shape, dtype) for dtype in scratch),
            pltpu.VMEM(shape, jnp.float32),
            pltpu.SemaphoreType.DMA((len(parts_of(shape[1])),)),
        ],
        compiler_params=PARAMS,
        name=name,
    )(*operands, *held)


def per_device(picture_embeds, caption_embeds, logit_multiplier, offset_shift):
    scalars = (logit_multiplier, offset_shift)
    odd, late = ((lax.axis_index(a) % 2).astype(jnp.int32)[None] for a in AXES)
    first = jnp.where(odd == FIRST, caption_embeds, picture_embeds)
    second = jnp.where(odd == FIRST, picture_embeds, caption_embeds)
    early_near = swapped(second, 0, 1 - FIRST, 0)
    first_far, first_near = swapped(first, 1, FIRST), swapped(first, 0, FIRST)
    second_far = swapped(second, 1, 1 - FIRST)
    late_near = swapped(second, 0, 1 - FIRST, 1)
    first_start, *second_own = own_call(*scalars, first, second, early_near)
    held = side_call(
        first_kernel,
        (*scalars, odd),
        (first, first_start, first_far, first_near),
        (),
        (),
        "first",
    )
    return side_call(
        second_kernel,
        (*scalars, odd, late),
        (second, *second_own, second_far, late_near),
        held,
        (jnp.bfloat16, jnp.float32),
        "second",
    )


def solution(mesh):
    placed = (P(("row", "col"), None), P(("row", "col"), None), P(), P())
    return jax.shard_map(
        per_device,
        mesh=mesh,
        in_specs=placed,
        out_specs=(P(("row", "col"), None), P(("row", "col"), None)),
        check_vma=False,
    )
```
